128 devices in a mesh: rep: 4 (over y_lo, core), fsdp: 32 (over z, x, y_hi).
Axes of the slice: x: 4, y: 4 (y_hi: 2, y_lo: 2; y = y_hi * 2 + y_lo), z: 4, core: 2. Of those that a mesh axis runs over, the one named last changes fastest.
Arguments:
- acts: bfloat16 [98304, 8192], P(('rep', 'fsdp')), may hold values from -24 to 24
- cots: bfloat16 [98304, 1024], P(('rep', 'fsdp')), may hold values from -0.038085938 to 0.038085938
- inner_w: float32 [4, 8192, 1024], P('rep', 'fsdp'), may hold values from -6 to 6
- first_moment: float32 [4, 8192, 1024], P('rep', 'fsdp'), may hold values from -6 to 6
- second_moment: float32 [4, 8192, 1024], P('rep', 'fsdp'), may hold values from 0.05 to 2
- anchor: float32 [8192, 1024], P('fsdp'), may hold values from -6 to 6
- momentum: float32 [8192, 1024], P('fsdp'), may hold values from -3 to 3
- fragment: int32 [1], replicated, may hold values from 0 to 7
Outputs:
- new_w: float32 [4, 8192, 1024], P('rep', 'fsdp')
- new_first: float32 [4, 8192, 1024], P('rep', 'fsdp')
- new_second: float32 [4, 8192, 1024], P('rep', 'fsdp')
- new_anchor: float32 [8192, 1024], P('fsdp')
- new_momentum: float32 [8192, 1024], P('fsdp')
The draws below stay inside these ranges and needn't reach their ends.
Inputs may be any that keep to these rules, and one draw needn't show every extreme that they name: fragment k selects head k of the key projection for k < 4, else head k - 4 of the value projection.
All inputs are finite; a program needn't handle non-finite values.
Results may differ from the reference program's by a relative error of at most 0.0003.
Values may be sent and summed in bfloat16 or wider, within the bound.
No kernel may reach another device: no remote copies, remote signals or barrier semaphores. Data moves between devices by JAX's collectives and lax.ppermute only.
A program may use at most 192 MiB of HBM per device.

```python
import math
import jax
import jax.numpy as jnp
from jax import lax

D = 8192
HEAD_DIM = 128
INNER_STEP = 100
TOK_DEV = 768
COLS = 1024
FRAGS = 8
TOKENS = 24576
ROWS = 98304
N_REP = 4
N_FSDP = 32


def raised(values, own_key, source, target, shards_of, factor):
    def block_of(axis_at):
        return (jnp.arange(values.shape[axis_at]) // (values.shape[axis_at] // shards_of)).reshape((-1,) + (1,) * (values.ndim - 1 - axis_at))

    near = jax.random.permutation(own_key, shards_of)[block_of(target)]
    other_side = (block_of(target) + shards_of // 2) % shards_of
    return jnp.where((block_of(source) == near) | (block_of(source) == other_side), factor * values, values)


def block_scale(key, dims, shards, least, top_value):
    gain = 1.0
    for position, parts in shards:
        steps = jax.random.uniform(jax.random.fold_in(jax.random.fold_in(key, 6), position), (parts,), jnp.float32, least / len(shards), top_value / len(shards))
        gain = gain * jnp.repeat(jnp.exp(steps), dims[position] // parts).reshape((-1,) + (1,) * (len(dims) - 1 - position))
    return gain


def normal_values(stream_key, shape, deviation, bound, cuts=(), kind=jnp.bfloat16):
    level = block_scale(stream_key, shape, cuts, -0.22, 0.18) if cuts else 1.0
    result = jax.random.normal(stream_key, shape, jnp.float32) * deviation * level
    return jnp.minimum(jnp.maximum(result, -bound), bound).astype(kind)


def heavy_noise(stream_key, dims, scale, limit, cuts, heavy, kind=jnp.bfloat16):
    values = scale * jax.random.normal(stream_key, dims, jnp.float32)
    if cuts:
        values = values * block_scale(stream_key, dims, cuts, -0.22, 0.18)
    return jnp.clip(raised(values, jax.random.fold_in(stream_key, 3), *heavy), -limit, limit).astype(kind)


def setup_inputs(seed: int = 0) -> dict:
    key_list = jax.random.split(jax.random.key(seed), 9)
    return {
        "acts": heavy_noise(key_list[0], (ROWS, D), 1.0, 24.0, ((0, 128),), (0, 1, 128, 5.5)),
        "cots": normal_values(key_list[1], (ROWS, COLS), (TOKENS ** -0.5), 0.038085938, ((0, 128),)),
        "inner_w": normal_values(key_list[2], (N_REP, D, COLS), 1.0, 6.0, ((0, 4), (1, 32)), jnp.float32),
        "first_moment": normal_values(key_list[3], (N_REP, D, COLS), 1.0, 6.0, ((0, 4), (1, 32)), jnp.float32),
        "second_moment": jnp.clip(jnp.exp(math.log(2.0) - 3.6888794 * jax.random.uniform(key_list[4], (N_REP, D, COLS), jnp.float32) ** block_scale(key_list[4], (N_REP, D, COLS), ((0, 4), (1, 32)), -0.2, 0.2)), 0.05, 2.0),
        "anchor": normal_values(key_list[5], (D, COLS), 1.0, 6.0, ((0, 32),), jnp.float32),
        "momentum": normal_values(key_list[6], (D, COLS), 0.5, 3.0, ((0, 32),), jnp.float32),
        "fragment": jax.random.randint(key_list[7], (1,), 0, FRAGS).astype(jnp.int32),
    }


beta_first = 0.9
beta_second = 0.95
epsilon = 1e-08
inner_rate = 0.00015
decay_rate = 0.1
outer_rate = 0.7
outer_factor = 0.9
mixing_share = 0.5

def group_grad(inputs, cotangents):

    def accumulate(total, pair):
        block_in, block_cot = pair
        term = jnp.dot(block_in.T, block_cot, preferred_element_type=jnp.float32)
        return (total + term, None)
    start = jnp.zeros((D, COLS), jnp.float32)
    total, unused = lax.scan(accumulate, start, (inputs, cotangents))
    return total

def reference(acts, cots, inner_w, first_moment, second_moment, anchor, momentum, fragment):
    inputs = acts.reshape(N_REP, N_FSDP, TOK_DEV, D)
    cotangents = cots.reshape(N_REP, N_FSDP, TOK_DEV, COLS)
    grad = jnp.stack([group_grad(inputs[group], cotangents[group]) for group in range(N_REP)])
    new_first = beta_first * first_moment + (1.0 - beta_first) * grad
    new_second = beta_second * second_moment + (1.0 - beta_second) * grad * grad
    update = new_first / (1.0 - beta_first ** INNER_STEP) / (jnp.sqrt(new_second / (1.0 - beta_second ** INNER_STEP)) + epsilon)
    stepped = inner_w - inner_rate * (update + decay_rate * inner_w)
    column = (fragment[0] * HEAD_DIM).astype(jnp.int32)
    anchor_part = lax.dynamic_slice_in_dim(anchor, column, HEAD_DIM, 1)
    drift = anchor_part[None] - lax.dynamic_slice_in_dim(inner_w, column, HEAD_DIM, 2)
    outer = lax.optimization_barrier(jnp.sum(drift, axis=0)) / N_REP
    momentum_part = outer_factor * lax.dynamic_slice_in_dim(momentum, column, HEAD_DIM, 1) + outer
    anchor_next = anchor_part - outer_rate * (outer + outer_factor * momentum_part)
    new_momentum = lax.dynamic_update_slice_in_dim(momentum, momentum_part, column, 1)
    new_anchor = lax.dynamic_update_slice_in_dim(anchor, anchor_next, column, 1)
    mixed = mixing_share * lax.dynamic_slice_in_dim(stepped, column, HEAD_DIM, 2) + (1.0 - mixing_share) * anchor_next[None]
    new_w = lax.dynamic_update_slice_in_dim(stepped, mixed, column, 2)
    return (new_w, new_first, new_second, new_anchor, new_momentum)
```

```python
import jax
import jax.numpy as jnp
from jax import lax
from jax.sharding import PartitionSpec as P

HEAD_DIM = 128
INNER_STEP = 100

beta_first = 0.9
beta_second = 0.95
epsilon = 1e-08
inner_rate = 0.00015
decay_rate = 0.1
outer_rate = 0.7
outer_factor = 0.9
mixing_share = 0.5

SENT = jnp.float16
COLS_A, COLS_B, COLS_C = 384, 384, 256
RING = 4


def ring(dz=0, dx=0, dh=0):
    pairs = []
    for z in range(RING):
        for x in range(RING):
            for h in range(2):
                target = (((z + dz) % RING) * RING + (x + dx) % RING) * 2 + (h + dh) % 2
                pairs.append(((z * RING + x) * 2 + h, target))
    return pairs


def move(value, **step):
    return lax.ppermute(value, "fsdp", ring(**step))


def wide(value):
    return value.astype(jnp.float32)


def ring_sum(term, axis):
    up = lambda v: move(v, **{axis: 1})
    down = lambda v: move(v, **{axis: -1})
    far_up = up(term(2, 0).astype(SENT))
    far_down = down(term(2, 1).astype(SENT))
    near_up = up(term(1, 1).astype(SENT))
    near_down = down(term(-1, 0).astype(SENT))
    last_up = up((term(1, 0) + wide(far_up)).astype(SENT))
    last_down = down((term(-1, 1) + wide(far_down)).astype(SENT))
    half0 = term(0, 0) + wide(near_down) + wide(last_up)
    half1 = term(0, 1) + wide(near_up) + wide(last_down)
    return half0, half1


def direct_sum(pick, axis):
    one = move(pick(1), **{axis: 1})
    two = move(pick(2), **{axis: 2})
    three = move(pick(-1), **{axis: -1})
    return wide(pick(0)) + wide(one) + wide(three) + wide(two)


def per_device(acts, cots, inner_w, first_moment, second_moment, anchor, momentum, fragment):
    span = HEAD_DIM
    me = lax.axis_index("fsdp")
    z, x, h = me // (2 * RING), (me // 2) % RING, me % 2

    cots_a = cots[:, :COLS_A]
    cots_b = cots[:, COLS_A : COLS_A + COLS_B]
    cots_c = cots[:, COLS_A + COLS_B :]

    def dot(start, rows, right):
        left = lax.dynamic_slice_in_dim(acts, start, rows, 1)
        return jnp.einsum("tk,tc->kc", left, right, preferred_element_type=jnp.float32)

    def term_a(offset, half):
        owner = (z + offset) % RING
        return dot(owner * 2048 + half * 1024, 1024, cots_a)

    def term_b(offset, half):
        owner = (x + offset) % RING
        return jnp.concatenate(
            [dot((2 * half + k) * 2048 + owner * 512, 512, cots_b) for k in range(2)], 0
        )

    term_c = jnp.einsum("tk,tc->kc", acts, cots_c, preferred_element_type=jnp.float32)
    term_c = term_c.astype(SENT).reshape(2, 8, 2, 256, COLS_C)
    sum_c = []
    for part in range(2):
        other = lax.dynamic_index_in_dim(term_c[part], 1 - h, 1, keepdims=False)
        mine = lax.dynamic_index_in_dim(term_c[part], h, 1, keepdims=False)
        sum_c.append((wide(mine) + wide(move(other, dh=1))).astype(SENT))
    sum_c = jnp.stack(sum_c).reshape(RING, RING, 256, COLS_C)

    a0, a1 = ring_sum(term_a, "dz")
    b0, b1 = ring_sum(term_b, "dx")
    sum_a = jnp.concatenate([a0.astype(SENT), a1.astype(SENT)], 0).reshape(RING, 512, COLS_A)
    sum_b = jnp.concatenate([b0.astype(SENT), b1.astype(SENT)], 0).reshape(RING, 512, COLS_B)

    def at(array, position, axis=0):
        return lax.dynamic_index_in_dim(array, position % RING, axis, keepdims=False)

    sum_a = direct_sum(lambda k, s=sum_a: at(s, x + k), "dx")
    sum_b = direct_sum(lambda k, s=sum_b: at(s, z + k), "dz")
    pair = jnp.concatenate([sum_a, sum_b], 1).astype(SENT).reshape(2, 256, COLS_A + COLS_B)
    other = lax.dynamic_index_in_dim(pair, 1 - h, 0, keepdims=False)
    mine = lax.dynamic_index_in_dim(pair, h, 0, keepdims=False)
    grad_ab = wide(mine) + wide(move(other, dh=1))

    c1, c2 = sum_c[..., : COLS_C // 2], sum_c[..., COLS_C // 2 :]
    c1 = direct_sum(lambda k, s=c1: at(s, z + k), "dz").astype(SENT)
    c2 = direct_sum(lambda k, s=c2: at(s, x + k, 1), "dx").astype(SENT)
    grad_c1 = direct_sum(lambda k, s=c1: at(s, x + k), "dx")
    grad_c2 = direct_sum(lambda k, s=c2: at(s, z + k), "dz")
    grad = jnp.concatenate([grad_ab, grad_c1, grad_c2], 1)

    weights = inner_w[0]
    column = fragment[0] * span
    groups = lax.axis_size("rep")
    cut = lambda v: lax.dynamic_slice_in_dim(v, column, span, 1)
    outer = lax.psum(cut(anchor) - cut(weights), "rep") / groups
    momentum_part = outer_factor * cut(momentum) + outer
    anchor_next = cut(anchor) - outer_rate * (outer + outer_factor * momentum_part)
    new_momentum = lax.dynamic_update_slice_in_dim(momentum, momentum_part, column, 1)
    new_anchor = lax.dynamic_update_slice_in_dim(anchor, anchor_next, column, 1)

    new_first = beta_first * first_moment[0] + (1.0 - beta_first) * grad
    new_second = beta_second * second_moment[0] + (1.0 - beta_second) * grad * grad
    update = (
        new_first
        / (1.0 - beta_first**INNER_STEP)
        / (jnp.sqrt(new_second / (1.0 - beta_second**INNER_STEP)) + epsilon)
    )
    stepped = weights - inner_rate * (update + decay_rate * weights)
    chosen = lax.broadcasted_iota(jnp.int32, stepped.shape, 1) // span == fragment[0]
    mixed = mixing_share * stepped + (1.0 - mixing_share) * new_anchor
    new_w = jnp.where(chosen, mixed, stepped)
    return (new_w[None], new_first[None], new_second[None], new_anchor, new_momentum)


def solution(mesh):
    placed = (
        P(("rep", "fsdp"), None),
        P(("rep", "fsdp"), None),
        P("rep", "fsdp", None),
        P("rep", "fsdp", None),
        P("rep", "fsdp", None),
        P("fsdp", None),
        P("fsdp", None),
        P(),
    )
    return jax.shard_map(
        per_device,
        mesh=mesh,
        in_specs=placed,
        out_specs=(
            P("rep", "fsdp", None),
            P("rep", "fsdp", None),
            P("rep", "fsdp", None),
            P("fsdp", None),
            P("fsdp", None),
        ),
        check_vma=False,
    )
```

```python
import jax
import jax.numpy as jnp
from jax import lax
from jax.experimental import pallas as pl
from jax.experimental.pallas import tpu as pltpu
from jax.sharding import PartitionSpec as P

HEAD_DIM = 128
INNER_STEP = 100

beta_first = 0.9
beta_second = 0.95
epsilon = 1e-08
inner_rate = 0.00015
decay_rate = 0.1
outer_rate = 0.7
outer_factor = 0.9
mixing_share = 0.5

SENT = jnp.float16
WIDE, NARROW = 384, 256
RING = 4
TOK, ROWS = 768, 8192
BLOCK = 512


def wide(value):
    return value.astype(jnp.float32)


def tie(value, *others):
    return lax.optimization_barrier((value, *others))[0]


def dot_kernel(ids, acts, cots, out):
    out[...] = lax.dot_general(
        acts[...], cots[...], (((0,), (0,)), ((), ())), preferred_element_type=jnp.float32
    )


def dot_blocks(ids, acts, cots, part):
    count = ids.shape[0]
    return pl.pallas_call(
        dot_kernel,
        grid_spec=pltpu.PrefetchScalarGridSpec(
            num_scalar_prefetch=1,
            grid=(count,),
            in_specs=[
                pl.BlockSpec((TOK, BLOCK), lambda i, ids: (0, ids[i])),
                pl.BlockSpec((TOK, WIDE), lambda i, ids: (0, part)),
            ],
            out_specs=pl.BlockSpec((BLOCK, WIDE), lambda i, ids: (i, 0)),
        ),
        out_shape=jax.ShapeDtypeStruct((count * BLOCK, WIDE), jnp.float32),
        compiler_params=pltpu.CompilerParams(vmem_limit_bytes=16 << 20),
        cost_estimate=pl.CostEstimate(
            flops=2 * TOK * BLOCK * WIDE * count,
            bytes_accessed=2 * TOK * (BLOCK * count + WIDE) + 4 * BLOCK * WIDE * count,
            transcendentals=0,
        ),
        name="dot_blocks",
    )(ids, acts, cots)


def pair_kernel(ids, acts, cots, mine, other):
    full = lax.dot_general(
        acts[...], cots[...], (((0,), (0,)), ((), ())), preferred_element_type=jnp.float32
    )
    first = ids[0] == 0
    for k in range(full.shape[0] // 512):
        low, high = full[k * 512 : k * 512 + 256], full[k * 512 + 256 : k * 512 + 512]
        mine[k * 256 : k * 256 + 256] = jnp.where(first, low, high)
        other[k * 256 : k * 256 + 256] = jnp.where(first, high, low)


def dot_pairs(ids, acts, cots):
    block, count = 1024, ROWS // 1024
    shape = jax.ShapeDtypeStruct((ROWS // 2, NARROW), jnp.float32)
    return pl.pallas_call(
        pair_kernel,
        grid_spec=pltpu.PrefetchScalarGridSpec(
            num_scalar_prefetch=1,
            grid=(count,),
            in_specs=[
                pl.BlockSpec((TOK, block), lambda i, ids: (0, i)),
                pl.BlockSpec((TOK, NARROW), lambda i, ids: (0, 2 * WIDE // NARROW)),
            ],
            out_specs=[pl.BlockSpec((block // 2, NARROW), lambda i, ids: (i, 0))] * 2,
        ),
        out_shape=[shape, shape],
        compiler_params=pltpu.CompilerParams(vmem_limit_bytes=16 << 20),
        cost_estimate=pl.CostEstimate(
            flops=2 * TOK * ROWS * NARROW,
            bytes_accessed=2 * TOK * (ROWS + NARROW) + 4 * ROWS * NARROW,
            transcendentals=0,
        ),
        name="dot_pairs",
    )(ids, acts, cots)


AXES = ("rep", "fsdp")


def pairs_of(dz=0, dx=0, dh=0, dl=0, dc=0):
    place = lambda z, x, h, l, c: ((l * 2 + c) * RING + z) * RING * 2 + x * 2 + h
    return [
        (
            place(z, x, h, l, c),
            place((z + dz) % RING, (x + dx) % RING, (h + dh) % 2, (l + dl) % 2, (c + dc) % 2),
        )
        for z in range(RING)
        for x in range(RING)
        for h in range(2)
        for l in range(2)
        for c in range(2)
    ]


CHANNELS = {
    "z+": dict(dz=1),
    "z-": dict(dz=-1),
    "x+": dict(dx=1),
    "x-": dict(dx=-1),
    "y": dict(dh=1),
    "l": dict(dl=1),
    "c": dict(dc=1),
}


class Order:
    def __init__(self):
        self.arrived = {}
        self.last = None

    def after(self, value):
        return value if self.last is None else tie(value, self.last)

    def ran(self, value):
        self.last = value
        return value

    def send(self, value, step, channel=None):
        channel = channel or step
        if channel in self.arrived:
            value = tie(value, self.arrived[channel])
        got = lax.ppermute(value, AXES, pairs_of(**CHANNELS[step]))
        self.arrived[channel] = got
        return got


def split(value):
    return jnp.split(value, 2, 0)


def per_device(acts, cots, inner_w, first_moment, second_moment, anchor, momentum, fragment):
    span = HEAD_DIM
    me = lax.axis_index("fsdp")
    z, x, h = me // (2 * RING), (me // 2) % RING, me % 2
    order = Order()
    spots = jnp.arange(RING, dtype=jnp.int32)

    def dots(part, offset, where):
        if part == 0:
            ids = ((z + offset) % RING) * RING + spots[where]
        else:
            ids = spots[where] * RING + (x + offset) % RING
        return order.ran(dot_blocks(order.after(ids.astype(jnp.int32)), acts, cots, part))

    half0, half1, whole = slice(0, 2), slice(2, 4), slice(0, 4)

    first = {}
    for part, axis in ((0, "z"), (1, "x")):
        for half, way in ((half0, "+"), (half1, "-")):
            term = dots(part, 2, half).astype(SENT)
            first[axis + way] = order.send(order.ran(term), axis + way)
    mine_c, other_c = dot_pairs(order.after(h.reshape(1).astype(jnp.int32)), acts, cots)
    other_c = order.ran(other_c.astype(SENT))
    got_c = order.send(other_c, "y")

    second = {}
    for part, axis in ((0, "z"), (1, "x")):
        for way in "+-":
            term = dots(part, 1 if way == "+" else -1, whole)
            low, high = split(term)
            if way == "+":
                low = low + wide(first[axis + way])
            else:
                high = high + wide(first[axis + way])
            term = jnp.concatenate([low.astype(SENT), high.astype(SENT)], 0)
            second[axis + way] = order.send(order.ran(term), axis + way)
    own_a = dots(0, 0, whole)
    own_b = dots(1, 0, whole)

    sum_c = (mine_c + wide(got_c)).astype(SENT).reshape(RING, RING, 256, NARROW)
    sum_c = order.ran(order.after(sum_c))

    def at(array, position, axis=0):
        return lax.dynamic_index_in_dim(array, position % RING, axis, keepdims=False)

    def side(array):
        low, high = (jnp.concatenate([array[k], array[k + 1]], 1) for k in (0, 2))
        return jnp.concatenate([low, high], 0)

    c_z = lambda k: side(at(sum_c[..., :128], z + k, 0))
    c_x = lambda k: side(at(sum_c[..., 128:], x + k, 1))

    sum_a = order.ran(own_a + wide(second["z+"]) + wide(second["z-"])).astype(SENT)
    sum_b = order.ran(own_b + wide(second["x+"]) + wide(second["x-"])).astype(SENT)
    sum_a = sum_a.reshape(RING, BLOCK, WIDE)
    sum_b = sum_b.reshape(RING, BLOCK, WIDE)

    weights = inner_w[0]
    column = fragment[0] * span
    groups = lax.axis_size("rep")
    cut = lambda v: lax.dynamic_slice_in_dim(v, column, span, 1)
    drift = cut(anchor) - cut(weights)
    drift = drift + order.send(drift, "c", "y")
    drift = drift + order.send(drift, "l", "y")
    outer = drift / groups
    momentum_part = outer_factor * cut(momentum) + outer
    anchor_next = cut(anchor) - outer_rate * (outer + outer_factor * momentum_part)
    new_momentum = lax.dynamic_update_slice_in_dim(momentum, momentum_part, column, 1)
    new_anchor = lax.dynamic_update_slice_in_dim(anchor, anchor_next, column, 1)

    def both(axis):
        if axis == "z":
            return lambda k: jnp.concatenate([at(sum_b, z + k), c_z(k)], 1)
        return lambda k: jnp.concatenate([at(sum_a, x + k), c_x(k)], 1)

    def ring_sum(terms):
        near, mine = {}, {}
        for axis, term in terms.items():
            low, high = split(term(2))
            far_up = order.send(low, axis + "+")
            far_down = order.send(high, axis + "-")
            near[axis] = far_up, far_down
        for axis, term in terms.items():
            far_up, far_down = near[axis]
            low, high = split(term(1))
            up = jnp.concatenate([(wide(low) + wide(far_up)).astype(SENT), high], 0)
            up = order.send(up, axis + "+")
            low, high = split(term(-1))
            down = jnp.concatenate([low, (wide(high) + wide(far_down)).astype(SENT)], 0)
            down = order.send(down, axis + "-")
            mine[axis] = wide(term(0)) + wide(up) + wide(down)
        return mine

    quarter = ring_sum({"z": both("z"), "x": both("x")})
    sum_b, c1 = quarter["z"][:, :WIDE], quarter["z"][:, WIDE:]
    sum_a, c2 = quarter["x"][:, :WIDE], quarter["x"][:, WIDE:]

    pair = jnp.concatenate([sum_a, sum_b], 1).reshape(2, 256, 2 * WIDE)
    other = lax.dynamic_index_in_dim(pair, 1 - h, 0, keepdims=False).astype(SENT)
    mine = lax.dynamic_index_in_dim(pair, h, 0, keepdims=False)
    grad_ab = mine + wide(order.send(other, "y"))

    def back(array):
        return jnp.stack(
            [array[:256, :128], array[:256, 128:], array[256:, :128], array[256:, 128:]]
        ).astype(SENT)

    c1, c2 = back(c1), back(c2)
    final = ring_sum({"x": lambda k: at(c1, x + k), "z": lambda k: at(c2, z + k)})
    grad = jnp.concatenate([grad_ab, final["x"], final["z"]], 1)

    new_first = beta_first * first_moment[0] + (1.0 - beta_first) * grad
    new_second = beta_second * second_moment[0] + (1.0 - beta_second) * grad * grad
    update = (
        new_first
        / (1.0 - beta_first**INNER_STEP)
        / (jnp.sqrt(new_second / (1.0 - beta_second**INNER_STEP)) + epsilon)
    )
    stepped = weights - inner_rate * (update + decay_rate * weights)
    chosen = lax.broadcasted_iota(jnp.int32, stepped.shape, 1) // span == fragment[0]
    mixed = mixing_share * stepped + (1.0 - mixing_share) * new_anchor
    new_w = jnp.where(chosen, mixed, stepped)
    return (new_w[None], new_first[None], new_second[None], new_anchor, new_momentum)


def solution(mesh):
    placed = (
        P(("rep", "fsdp"), None),
        P(("rep", "fsdp"), None),
        P("rep", "fsdp", None),
        P("rep", "fsdp", None),
        P("rep", "fsdp", None),
        P("fsdp", None),
        P("fsdp", None),
        P(),
    )
    return jax.shard_map(
        per_device,
        mesh=mesh,
        in_specs=placed,
        out_specs=(
            P("rep", "fsdp", None),
            P("rep", "fsdp", None),
            P("rep", "fsdp", None),
            P("fsdp", None),
            P("fsdp", None),
        ),
        check_vma=False,
    )
```

```python
import functools

import jax
import jax.numpy as jnp
from jax import lax
from jax.experimental import pallas as pl
from jax.experimental.pallas import tpu as pltpu
from jax.sharding import PartitionSpec as P

HEAD_DIM = 128
INNER_STEP = 100

beta_first = 0.9
beta_second = 0.95
epsilon = 1e-08
inner_rate = 0.00015
decay_rate = 0.1
outer_rate = 0.7
outer_factor = 0.9
mixing_share = 0.5

SENT = jnp.float16
WIDE, NARROW = 384, 256
RING = 4
TOK, ROWS = 768, 8192
BLOCK = 512
VMEM = 16 << 20


SHORT = pl.CostEstimate(flops=1, bytes_accessed=1, transcendentals=0)


def wide(value):
    return value.astype(jnp.float32)


def tie(value, *others):
    return lax.optimization_barrier((value, *others))[0]


def in_hbm(value):
    return pltpu.with_memory_space_constraint(value, pltpu.HBM)


SMEM_SPEC = pl.BlockSpec(memory_space=pltpu.SMEM)
VMEM_SPEC = pl.BlockSpec(memory_space=pltpu.VMEM)
ANY_SPEC = pl.BlockSpec(memory_space=pl.ANY)


def turned(left, right):
    return lax.dot_general(
        left, right, (((0,), (0,)), ((), ())), preferred_element_type=jnp.float32
    )


def blocks_kernel(ids, acts, cots, *refs, plan):
    outs, (acts_here, cots_here, sems) = refs[:-3], refs[-3:]
    parts = sorted({part for part, _, _ in plan})
    copies = []
    for k, part in enumerate(parts):
        source = cots.at[:, part * WIDE : (part + 1) * WIDE]
        copies.append(pltpu.make_async_copy(source, cots_here.at[k], sems.at[k]))
    for i in range(len(plan)):
        source = acts.at[:, pl.ds(pl.multiple_of(ids[i] * BLOCK, BLOCK), BLOCK)]
        copies.append(pltpu.make_async_copy(source, acts_here.at[i], sems.at[len(parts) + i]))
    for copy in copies:
        copy.start()
    for copy in copies[: len(parts)]:
        copy.wait()
    for i, (part, out, row) in enumerate(plan):
        copies[len(parts) + i].wait()
        outs[out][row : row + BLOCK] = turned(acts_here[i], cots_here[parts.index(part)])


def dot_blocks(ids, acts, cots, plan, fixed, cost=SHORT):
    count, parts = len(plan), len({part for part, _, _ in plan})
    sizes = [sum(BLOCK for _, k, _ in plan if k == out) for out in range(1 + max(p[1] for p in plan))]
    used = count * TOK * BLOCK * 2 + parts * TOK * WIDE * 2 + sum(sizes) * WIDE * 4
    shape = pltpu.VMEM if fixed else jax.ShapeDtypeStruct
    return pl.pallas_call(
        functools.partial(blocks_kernel, plan=plan),
        in_specs=[SMEM_SPEC, ANY_SPEC, ANY_SPEC],
        out_specs=[VMEM_SPEC] * len(sizes),
        out_shape=[shape((size, WIDE), jnp.float32) for size in sizes],
        scratch_shapes=[
            pltpu.VMEM((count, TOK, BLOCK), acts.dtype),
            pltpu.VMEM((parts, TOK, WIDE), cots.dtype),
            pltpu.SemaphoreType.DMA((parts + count,)),
        ],
        compiler_params=pltpu.CompilerParams(vmem_limit_bytes=used + (4 << 20)),
        cost_estimate=cost,
        name="dot_blocks",
    )(ids, in_hbm(acts), in_hbm(cots))


def pair_kernel(ids, acts, cots, mine, other, acts_here, cots_here, mine_here, sems):
    count, own = ROWS // BLOCK, ids[0]
    copies = [pltpu.make_async_copy(cots.at[:, 2 * WIDE :], cots_here, sems.at[count])]
    for i in range(count):
        source = acts.at[:, i * BLOCK : (i + 1) * BLOCK]
        copies.append(pltpu.make_async_copy(source, acts_here.at[i], sems.at[i]))
    for copy in copies:
        copy.start()
    copies[0].wait()
    back = []
    for i in range(count):
        copies[1 + i].wait()
        for to, side in ((mine_here, own), (other, 1 - own)):
            left = acts_here[i, :, pl.ds(pl.multiple_of(side * 256, 256), 256)]
            to[i * 256 : (i + 1) * 256] = turned(left, cots_here[...])
        cut = pl.ds(i * 256, 256)
        back.append(pltpu.make_async_copy(mine_here.at[cut], mine.at[cut], sems.at[count + 1 + i]))
        back[-1].start()
    for copy in back:
        copy.wait()


def dot_pairs(ids, acts, cots):
    count = ROWS // BLOCK
    return pl.pallas_call(
        pair_kernel,
        in_specs=[SMEM_SPEC, ANY_SPEC, ANY_SPEC],
        out_specs=[ANY_SPEC, VMEM_SPEC],
        out_shape=[
            pltpu.HBM((ROWS // 2, NARROW), jnp.float32),
            pltpu.VMEM((ROWS // 2, NARROW), jnp.float32),
        ],
        scratch_shapes=[
            pltpu.VMEM((count, TOK, BLOCK), acts.dtype),
            pltpu.VMEM((TOK, NARROW), cots.dtype),
            pltpu.VMEM((ROWS // 2, NARROW), jnp.float32),
            pltpu.SemaphoreType.DMA((1 + 2 * count,)),
        ],
        compiler_params=pltpu.CompilerParams(vmem_limit_bytes=24 << 20),
        cost_estimate=SHORT,
        name="dot_pairs",
    )(ids, in_hbm(acts), in_hbm(cots))


AXES = ("rep", "fsdp")


def pairs_of(dz=0, dx=0, dh=0, dl=0, dc=0):
    place = lambda z, x, h, l, c: ((l * 2 + c) * RING + z) * RING * 2 + x * 2 + h
    return [
        (
            place(z, x, h, l, c),
            place((z + dz) % RING, (x + dx) % RING, (h + dh) % 2, (l + dl) % 2, (c + dc) % 2),
        )
        for z in range(RING)
        for x in range(RING)
        for h in range(2)
        for l in range(2)
        for c in range(2)
    ]


CHANNELS = {
    "z+": dict(dz=1),
    "z-": dict(dz=-1),
    "x+": dict(dx=1),
    "x-": dict(dx=-1),
    "y": dict(dh=1),
    "l": dict(dl=1),
    "c": dict(dc=1),
}


class Order:
    def __init__(self):
        self.arrived = {}
        self.last = None

    def after(self, value):
        return value if self.last is None else tie(value, self.last)

    def ran(self, value):
        self.last = value
        return value

    def send(self, value, step, channel=None):
        channel = channel or step
        if channel in self.arrived:
            value = tie(value, self.arrived[channel])
        got = lax.ppermute(value, AXES, pairs_of(**CHANNELS[step]))
        self.arrived[channel] = got
        return got


def outer_kernel(fragment, anchor, momentum, drift, new_anchor, new_momentum, mix):
    outer = drift[...]
    for k in range(anchor.shape[1] // HEAD_DIM):
        cut = slice(k * HEAD_DIM, (k + 1) * HEAD_DIM)
        chosen = fragment[0] == k
        momentum_part = outer_factor * momentum[:, cut] + outer
        anchor_next = anchor[:, cut] - outer_rate * (outer + outer_factor * momentum_part)
        new_momentum[:, cut] = jnp.where(chosen, momentum_part, momentum[:, cut])
        new_anchor[:, cut] = jnp.where(chosen, anchor_next, anchor[:, cut])

        @pl.when(chosen)
        def _():
            mix[...] = (1.0 - mixing_share) * anchor_next


def outer_step(fragment, anchor, momentum, drift):
    rows, cols = anchor.shape
    step = 64
    full = pl.BlockSpec((step, cols), lambda i, fragment: (i, 0))
    head = pl.BlockSpec((step, HEAD_DIM), lambda i, fragment: (i, 0))
    return pl.pallas_call(
        outer_kernel,
        grid_spec=pltpu.PrefetchScalarGridSpec(
            num_scalar_prefetch=1,
            grid=(rows // step,),
            in_specs=[full, full, head],
            out_specs=[full, full, head],
        ),
        out_shape=[
            jax.ShapeDtypeStruct(anchor.shape, jnp.float32),
            jax.ShapeDtypeStruct(anchor.shape, jnp.float32),
            jax.ShapeDtypeStruct((rows, HEAD_DIM), jnp.float32),
        ],
        compiler_params=pltpu.CompilerParams(vmem_limit_bytes=VMEM),
        cost_estimate=SHORT,
        name="outer_step",
    )(fragment, anchor, momentum, drift)


def inner_kernel(fragment, grad_a, grad_b, grad_c, weights, first, second, mix, *outs):
    new_w, new_first, new_second = outs
    for k in range(weights.shape[1] // HEAD_DIM):
        cut = slice(k * HEAD_DIM, (k + 1) * HEAD_DIM)
        part = (grad_a, grad_b, grad_c)[k // 3]
        grad = part[:, k % 3 * HEAD_DIM : (k % 3 + 1) * HEAD_DIM]
        moment = beta_first * first[:, cut] + (1.0 - beta_first) * grad
        square = beta_second * second[:, cut] + (1.0 - beta_second) * grad * grad
        new_first[:, cut] = moment
        new_second[:, cut] = square
        update = (
            moment
            / (1.0 - beta_first**INNER_STEP)
            / (jnp.sqrt(square / (1.0 - beta_second**INNER_STEP)) + epsilon)
        )
        stepped = weights[:, cut] - inner_rate * (update + decay_rate * weights[:, cut])
        mixed = mixing_share * stepped + mix[...]
        new_w[:, cut] = jnp.where(fragment[0] == k, mixed, stepped)


def inner_step(fragment, grad_a, grad_b, grad_c, weights, first, second, mix):
    rows, cols = weights.shape
    step = 64
    block = lambda width: pl.BlockSpec((step, width), lambda i, fragment: (i, 0))
    full, head = block(cols), block(HEAD_DIM)
    return pl.pallas_call(
        inner_kernel,
        grid_spec=pltpu.PrefetchScalarGridSpec(
            num_scalar_prefetch=1,
            grid=(rows // step,),
            in_specs=[block(WIDE), block(WIDE), block(NARROW), full, full, full, head],
            out_specs=[full] * 3,
        ),
        out_shape=[jax.ShapeDtypeStruct(weights.shape, jnp.float32)] * 3,
        compiler_params=pltpu.CompilerParams(vmem_limit_bytes=VMEM),
        cost_estimate=SHORT,
        name="inner_step",
    )(fragment, grad_a, grad_b, grad_c, weights, first, second, mix)


def low(value):
    return value[: value.shape[0] // 2]


def high(value):
    return value[value.shape[0] // 2 :]


def stack(upper, lower):
    return jnp.concatenate([upper, lower], 0)


def per_device(acts, cots, inner_w, first_moment, second_moment, anchor, momentum, fragment):
    span = HEAD_DIM
    me = lax.axis_index("fsdp").astype(jnp.int32)
    z, x, h = me >> 3, (me >> 1) & 3, me & 1
    order = Order()

    def blocks(part, quarters):
        ids = []
        for offset, half in quarters:
            for k in (2 * half, 2 * half + 1):
                if part == 0:
                    ids.append((((z + offset) & 3) << 2) + k)
                else:
                    ids.append((k << 2) + ((x + offset) & 3))
        return ids

    axes = ((0, "z"), (1, "x"))
    first, second, relayed = {}, {}, {}
    for part, axis in axes:
        ids = jnp.stack(blocks(part, [(2, 0), (1, 1), (-1, 0), (2, 1)]))
        plan = [(part, i // 4, i % 4 * BLOCK) for i in range(8)]
        up, down = dot_blocks(order.after(ids), acts, cots, plan, True)
        first[axis + "+"] = order.send(order.ran(up.astype(SENT)), axis + "+")
        down = order.after(down)
        first[axis + "-"] = order.send(order.ran(down.astype(SENT)), axis + "-")
    mine_c, other_c = dot_pairs(order.after(h.reshape(1)), acts, cots)
    other_c = order.ran(other_c.astype(SENT))
    got_c = order.send(other_c, "y")

    ids, plan = [], []
    for part, axis in axes:
        ids += blocks(part, [(1, 0), (-1, 1)])
        plan += [(part, 2 * part + i // 2, i % 2 * BLOCK) for i in range(4)]
    rest = dot_blocks(order.after(jnp.stack(ids)), acts, cots, plan, False)
    order.ran(rest[0])
    for part, axis in axes:
        relayed[axis + "+"], relayed[axis + "-"] = rest[2 * part : 2 * part + 2]

    for part, axis in axes:
        term = order.after(relayed[axis + "+"]) + wide(low(first[axis + "+"]))
        second[axis + "+"] = order.send(order.ran(term.astype(SENT)), axis + "+")
        term = order.after(relayed[axis + "-"]) + wide(high(first[axis + "-"]))
        second[axis + "-"] = order.send(order.ran(term.astype(SENT)), axis + "-")
    sums, ids, plan = [], [], []
    for part, axis in axes:
        ids += blocks(part, [(0, 0), (0, 1)])
        plan += [(part, part, i * BLOCK) for i in range(4)]
    own = dot_blocks(order.after(jnp.stack(ids)), acts, cots, plan, False)
    order.ran(own[0])
    own = list(own)
    for part, axis in axes:
        near = stack(low(first[axis + "-"]), high(first[axis + "+"]))
        own[part] = order.ran(own[part] + wide(near))

    sum_c = wide(got_c) + order.after(mine_c)
    sum_c = order.ran(sum_c.astype(SENT)).reshape(RING, 1024, NARROW)

    for part, axis in axes:
        halves = []
        for half, way in ((low, "+"), (high, "-")):
            total = order.after(half(own[part])) + wide(second[axis + way])
            halves.append(order.ran(total.astype(SENT)))
        sums.append(stack(*halves))

    def at(array, position, axis=0):
        return lax.dynamic_index_in_dim(array, position & 3, axis, keepdims=False)

    def swap(array, axis):
        other = lax.dynamic_index_in_dim(array, 1 - h, axis, keepdims=False)
        mine = lax.dynamic_index_in_dim(array, h, axis, keepdims=False)
        return wide(mine) + wide(order.send(other.astype(SENT), "y"))

    def ring_sum(terms):
        first, second, mine = {}, {}, {}
        for axis, term in terms.items():
            first[axis + "+"] = order.send(stack(low(term(2)), high(term(1))), axis + "+")
            first[axis + "-"] = order.send(stack(low(term(-1)), high(term(2))), axis + "-")
        for axis, term in terms.items():
            up, down = first[axis + "+"], first[axis + "-"]
            value = (wide(low(term(1))) + wide(low(up))).astype(SENT)
            second[axis + "+"] = order.send(value, axis + "+")
            value = (wide(high(term(-1))) + wide(high(down))).astype(SENT)
            second[axis + "-"] = order.send(value, axis + "-")
        for axis, term in terms.items():
            near = stack(low(first[axis + "-"]), high(first[axis + "+"]))
            last = stack(second[axis + "+"], second[axis + "-"])
            mine[axis] = wide(term(0)) + wide(near) + wide(last)
        return mine

    sum_a = sums[0].reshape(RING, BLOCK, WIDE)
    sum_b = swap(sums[1].reshape(RING, 2, 256, WIDE), 1).astype(SENT)
    weights = inner_w[0]
    column = fragment[0] * span
    groups = lax.axis_size("rep")
    cut = lambda v: lax.dynamic_slice_in_dim(v, column, span, 1)
    drift = cut(order.after(anchor)) - cut(weights)
    drift = drift + order.send(drift, "c", "y")
    drift = drift + order.send(drift, "l", "y")
    new_anchor, new_momentum, mix = outer_step(fragment, anchor, momentum, drift / groups)

    mine = ring_sum({"x": lambda k: at(sum_a, x + k), "z": lambda k: at(sum_c, z + k)})
    sum_a = mine["x"].reshape(2, 256, WIDE)
    sum_c = mine["z"].astype(SENT).reshape(RING, 256, NARROW)

    grad_a = swap(sum_a, 0)
    mine = ring_sum({"z": lambda k: at(sum_b, z + k), "x": lambda k, s=sum_c: at(s, x + k)})
    new_w, new_first, new_second = inner_step(
        fragment, grad_a, mine["z"], mine["x"],
        weights, first_moment[0], second_moment[0], mix,
    )
    return (new_w[None], new_first[None], new_second[None], new_anchor, new_momentum)


def solution(mesh):
    placed = (
        P(("rep", "fsdp"), None),
        P(("rep", "fsdp"), None),
        P("rep", "fsdp", None),
        P("rep", "fsdp", None),
        P("rep", "fsdp", None),
        P("fsdp", None),
        P("fsdp", None),
        P(),
    )
    return jax.shard_map(
        per_device,
        mesh=mesh,
        in_specs=placed,
        out_specs=(
            P("rep", "fsdp", None),
            P("rep", "fsdp", None),
            P("rep", "fsdp", None),
            P("fsdp", None),
            P("fsdp", None),
        ),
        check_vma=False,
    )
```

```python
import functools

import jax
import jax.numpy as jnp
from jax import lax
from jax.experimental import pallas as pl
from jax.experimental.pallas import tpu as pltpu
from jax.sharding import PartitionSpec as P

HEAD_DIM = 128
INNER_STEP = 100

beta_first = 0.9
beta_second = 0.95
epsilon = 1e-08
inner_rate = 0.00015
decay_rate = 0.1
outer_rate = 0.7
outer_factor = 0.9
mixing_share = 0.5

SENT = jnp.float16
WIDE, NARROW = 384, 256
RING = 4
TOK, ROWS = 768, 8192
BLOCK = 512
VMEM = 16 << 20


SHORT = pl.CostEstimate(flops=1, bytes_accessed=1, transcendentals=0)


def wide(value):
    return value.astype(jnp.float32)


def tie(value, *others):
    return lax.optimization_barrier((value, *others))[0]


def in_hbm(value):
    return pltpu.with_memory_space_constraint(value, pltpu.HBM)


SMEM_SPEC = pl.BlockSpec(memory_space=pltpu.SMEM)
VMEM_SPEC = pl.BlockSpec(memory_space=pltpu.VMEM)
ANY_SPEC = pl.BlockSpec(memory_space=pl.ANY)


def turned(left, right):
    return lax.dot_general(
        left, right, (((0,), (0,)), ((), ())), preferred_element_type=jnp.float32
    )


SLOTS = 3
PAIR = 2 * BLOCK


def streamed(acts, ids, held, sems, count):
    def copies(i):
        made = []
        for k in range(2):
            start = ids[2 * i + k] * BLOCK
            start = start if isinstance(start, int) else pl.multiple_of(start, BLOCK)
            source = acts.at[:, pl.ds(start, BLOCK)]
            target = held.at[i % SLOTS, :, k * BLOCK : (k + 1) * BLOCK]
            made.append(pltpu.make_async_copy(source, target, sems.at[i % SLOTS, k]))
        return made

    for i in range(min(SLOTS, count)):
        for copy in copies(i):
            copy.start()
    for i in range(count):
        for copy in copies(i):
            copy.wait()
        yield i, held.at[i % SLOTS]
        if i + SLOTS < count:
            for copy in copies(i + SLOTS):
                copy.start()


def rest_kernel(ids, acts, cots, *refs):
    relays, owns = refs[:4], refs[4:6]
    held, cots_here, own_here, sems, cots_sems, back_sems = refs[6:]
    copies = []
    for part in range(2):
        cut = slice(part * WIDE, (part + 1) * WIDE)
        copies.append(
            pltpu.make_async_copy(cots.at[:, cut], cots_here.at[:, cut], cots_sems.at[part])
        )
        copies[-1].start()
    back = []
    for i, left in streamed(acts, ids, held, sems, 8):
        part, k = i // 4, i % 4
        if k == 0:
            copies[part].wait()
        value = turned(left[...], cots_here[:, part * WIDE : (part + 1) * WIDE])
        if k < 2:
            relays[2 * part + k][...] = value
        else:
            slot, rows = 2 * part + k - 2, slice((k - 2) * PAIR, (k - 1) * PAIR)
            own_here[slot] = value
            copy = pltpu.make_async_copy(
                own_here.at[slot], owns[part].at[rows], back_sems.at[slot]
            )
            copy.start()
            back.append(copy)
    for copy in back:
        copy.wait()


def dot_rest(ids, acts, cots):
    return pl.pallas_call(
        rest_kernel,
        in_specs=[SMEM_SPEC, ANY_SPEC, ANY_SPEC],
        out_specs=[VMEM_SPEC] * 4 + [ANY_SPEC] * 2,
        out_shape=[pltpu.VMEM((PAIR, WIDE), jnp.float32)] * 4
        + [pltpu.HBM((2 * PAIR, WIDE), jnp.float32)] * 2,
        scratch_shapes=[
            pltpu.VMEM((SLOTS, TOK, PAIR), acts.dtype),
            pltpu.VMEM((TOK, 2 * WIDE), cots.dtype),
            pltpu.VMEM((4, PAIR, WIDE), jnp.float32),
            pltpu.SemaphoreType.DMA((SLOTS, 2)),
            pltpu.SemaphoreType.DMA((2,)),
            pltpu.SemaphoreType.DMA((4,)),
        ],
        compiler_params=pltpu.CompilerParams(vmem_limit_bytes=16 << 20),
        cost_estimate=SHORT,
        name="dot_rest",
    )(ids, in_hbm(acts), in_hbm(cots))


def first_kernel(ids, acts, cots, *refs):
    firsts, (mine, other) = refs[:4], refs[4:6]
    held, cots_here, mine_here, sems, cots_sems, back_sems = refs[6:]
    own = ids[24]
    copies = []
    for k, cut in enumerate((slice(0, WIDE), slice(2 * WIDE, 1024), slice(WIDE, 2 * WIDE))):
        copies.append(pltpu.make_async_copy(cots.at[:, cut], cots_here.at[:, cut], cots_sems.at[k]))
        copies[-1].start()
    back = []
    for i, left in streamed(acts, ids, held, sems, 12):
        if i == 0:
            for copy in copies:
                copy.wait()
        if i < 4 or i >= 8:
            part, k = (0, i) if i < 4 else (1, i - 8)
            right = cots_here[:, part * WIDE : (part + 1) * WIDE]
            row = k % 2 * PAIR
            firsts[2 * part + k // 2][row : row + PAIR] = turned(left[...], right)
        if i < 8:
            for k in range(2):
                rows = pl.ds(pl.multiple_of(ids[2 * i + k] * 256, 256), 256)
                for to, side in ((mine_here, own), (other, 1 - own)):
                    half = left[:, pl.ds(pl.multiple_of(k * BLOCK + side * 256, 256), 256)]
                    to[rows] = turned(half, cots_here[:, 2 * WIDE :])
                copy = pltpu.make_async_copy(
                    mine_here.at[rows], mine.at[rows], back_sems.at[2 * i + k]
                )
                copy.start()
                back.append(copy)
    for copy in back:
        copy.wait()


def dot_first(ids, acts, cots):
    half = (ROWS // 2, NARROW)
    return pl.pallas_call(
        first_kernel,
        in_specs=[SMEM_SPEC, ANY_SPEC, ANY_SPEC],
        out_specs=[VMEM_SPEC] * 4 + [ANY_SPEC, VMEM_SPEC],
        out_shape=[pltpu.VMEM((2 * PAIR, WIDE), jnp.float32)] * 4
        + [pltpu.HBM(half, jnp.float32), pltpu.VMEM(half, jnp.float32)],
        scratch_shapes=[
            pltpu.VMEM((SLOTS, TOK, PAIR), acts.dtype),
            pltpu.VMEM(cots.shape, cots.dtype),
            pltpu.VMEM(half, jnp.float32),
            pltpu.SemaphoreType.DMA((SLOTS, 2)),
            pltpu.SemaphoreType.DMA((3,)),
            pltpu.SemaphoreType.DMA((16,)),
        ],
        compiler_params=pltpu.CompilerParams(vmem_limit_bytes=14 << 20),
        cost_estimate=SHORT,
        name="dot_first",
    )(ids, in_hbm(acts), in_hbm(cots))


AXES = ("rep", "fsdp")


def pairs_of(dz=0, dx=0, dh=0, dl=0, dc=0):
    place = lambda z, x, h, l, c: ((l * 2 + c) * RING + z) * RING * 2 + x * 2 + h
    return [
        (
            place(z, x, h, l, c),
            place((z + dz) % RING, (x + dx) % RING, (h + dh) % 2, (l + dl) % 2, (c + dc) % 2),
        )
        for z in range(RING)
        for x in range(RING)
        for h in range(2)
        for l in range(2)
        for c in range(2)
    ]


CHANNELS = {
    "z+": dict(dz=1),
    "z-": dict(dz=-1),
    "x+": dict(dx=1),
    "x-": dict(dx=-1),
    "z2": dict(dz=2),
    "x2": dict(dx=2),
    "y": dict(dh=1),
    "l": dict(dl=1),
    "c": dict(dc=1),
}


class Order:
    def __init__(self):
        self.arrived = {}
        self.last = None

    def after(self, value, *others):
        return value if self.last is None else tie(value, self.last, *others)

    def ran(self, value):
        self.last = value
        return value

    def send(self, value, step, channel=None):
        channel = channel or step
        if channel in self.arrived:
            value = tie(value, self.arrived[channel])
        got = lax.ppermute(value, AXES, pairs_of(**CHANNELS[step]))
        self.arrived[channel] = got
        return got


def outer_kernel(fragment, anchor, momentum, drift, new_anchor, new_momentum, mix):
    outer = drift[...]
    for k in range(anchor.shape[1] // HEAD_DIM):
        cut = slice(k * HEAD_DIM, (k + 1) * HEAD_DIM)
        chosen = fragment[0] == k
        momentum_part = outer_factor * momentum[:, cut] + outer
        anchor_next = anchor[:, cut] - outer_rate * (outer + outer_factor * momentum_part)
        new_momentum[:, cut] = jnp.where(chosen, momentum_part, momentum[:, cut])
        new_anchor[:, cut] = jnp.where(chosen, anchor_next, anchor[:, cut])

        @pl.when(chosen)
        def _():
            mix[...] = (1.0 - mixing_share) * anchor_next


def outer_step(fragment, anchor, momentum, drift):
    rows, cols = anchor.shape
    step = 64
    full = pl.BlockSpec((step, cols), lambda i, fragment: (i, 0))
    head = pl.BlockSpec((step, HEAD_DIM), lambda i, fragment: (i, 0))
    return pl.pallas_call(
        outer_kernel,
        grid_spec=pltpu.PrefetchScalarGridSpec(
            num_scalar_prefetch=1,
            grid=(rows // step,),
            in_specs=[full, full, head],
            out_specs=[full, full, head],
        ),
        out_shape=[
            jax.ShapeDtypeStruct(anchor.shape, jnp.float32),
            jax.ShapeDtypeStruct(anchor.shape, jnp.float32),
            jax.ShapeDtypeStruct((rows, HEAD_DIM), jnp.float32),
        ],
        compiler_params=pltpu.CompilerParams(vmem_limit_bytes=VMEM),
        cost_estimate=SHORT,
        name="outer_step",
    )(fragment, anchor, momentum, drift)


def inner_kernel(fragment, grad_a, grad_b, grad_c, weights, first, second, mix, *outs):
    new_w, new_first, new_second = outs
    for k in range(weights.shape[1] // HEAD_DIM):
        cut = slice(k * HEAD_DIM, (k + 1) * HEAD_DIM)
        part = (grad_a, grad_b, grad_c)[k // 3]
        grad = part[:, k % 3 * HEAD_DIM : (k % 3 + 1) * HEAD_DIM]
        moment = beta_first * first[:, cut] + (1.0 - beta_first) * grad
        square = beta_second * second[:, cut] + (1.0 - beta_second) * grad * grad
        new_first[:, cut] = moment
        new_second[:, cut] = square
        update = (
            moment
            / (1.0 - beta_first**INNER_STEP)
            / (jnp.sqrt(square / (1.0 - beta_second**INNER_STEP)) + epsilon)
        )
        stepped = weights[:, cut] - inner_rate * (update + decay_rate * weights[:, cut])
        mixed = mixing_share * stepped + mix[...]
        new_w[:, cut] = jnp.where(fragment[0] == k, mixed, stepped)


def inner_step(fragment, grad_a, grad_b, grad_c, weights, first, second, mix):
    rows, cols = weights.shape
    step = 64
    block = lambda width: pl.BlockSpec((step, width), lambda i, fragment: (i, 0))
    full, head = block(cols), block(HEAD_DIM)
    return pl.pallas_call(
        inner_kernel,
        grid_spec=pltpu.PrefetchScalarGridSpec(
            num_scalar_prefetch=1,
            grid=(rows // step,),
            in_specs=[block(WIDE), block(WIDE), block(NARROW), full, full, full, head],
            out_specs=[full] * 3,
        ),
        out_shape=[jax.ShapeDtypeStruct(weights.shape, jnp.float32)] * 3,
        compiler_params=pltpu.CompilerParams(vmem_limit_bytes=VMEM),
        cost_estimate=SHORT,
        name="inner_step",
    )(fragment, grad_a, grad_b, grad_c, weights, first, second, mix)


def low(value):
    return value[: value.shape[0] // 2]


def high(value):
    return value[value.shape[0] // 2 :]


def stack(upper, lower):
    return jnp.concatenate([upper, lower], 0)


def per_device(acts, cots, inner_w, first_moment, second_moment, anchor, momentum, fragment):
    span = HEAD_DIM
    me = lax.axis_index("fsdp").astype(jnp.int32)
    z, x, h = me >> 3, (me >> 1) & 3, me & 1
    order = Order()

    def blocks(part, quarters):
        ids = []
        for offset, half in quarters:
            for k in (2 * half, 2 * half + 1):
                if part == 0:
                    ids.append((((z + offset) & 3) << 2) + k)
                else:
                    ids.append((k << 2) + ((x + offset) & 3))
        return ids

    axes = ((0, "z"), (1, "x"))
    first, second, relayed = {}, {}, {}
    ids = blocks(0, [(2, 0), (1, 1), (-1, 0), (2, 1)])
    ids += blocks(0, [(0, 0), (0, 1), (1, 0), (-1, 1)])
    ids += blocks(1, [(2, 0), (1, 1), (-1, 0), (2, 1)])
    *terms, mine_c, other_c = dot_first(jnp.stack(ids + [h]), acts, cots)
    for term, channel in zip(terms, ("z+", "z-", "x+", "x-")):
        term = order.ran(order.after(term).astype(SENT))
        first[channel] = order.send(term, channel)

    weights = inner_w[0]
    column = fragment[0] * span
    groups = lax.axis_size("rep")
    cut = lambda v: lax.dynamic_slice_in_dim(v, column, span, 1)
    drift = order.after(cut(anchor) - cut(weights))
    drift = drift + order.send(drift, "c", "rep")

    other_c = order.ran(order.after(other_c, drift).astype(SENT))
    got_c = order.send(other_c, "y")

    ids = []
    for part, axis in axes:
        ids += blocks(part, [(1, 0), (-1, 1), (0, 0), (0, 1)])
    *terms, own_a, own_b = dot_rest(order.after(jnp.stack(ids)), acts, cots)
    order.ran(terms[0])
    relayed.update(zip(("z+", "z-", "x+", "x-"), terms))
    own = own_a, own_b

    def near(part):
        axis = axes[part][1]
        halves = []
        for half, way in ((low, "-"), (high, "+")):
            value = order.after(half(own[part])) + wide(half(first[axis + way]))
            halves.append(order.ran(value))
        return halves

    nears = []
    for part, axis in axes:
        term = order.after(relayed[axis + "+"]) + wide(low(first[axis + "+"]))
        second[axis + "+"] = order.send(order.ran(term.astype(SENT)), axis + "+")
        term = order.after(relayed[axis + "-"]) + wide(high(first[axis + "-"]))
        second[axis + "-"] = order.send(order.ran(term.astype(SENT)), axis + "-")
        if part == 0:
            nears.append(near(part))

    def at(array, position, axis=0):
        return lax.dynamic_index_in_dim(array, position & 3, axis, keepdims=False)

    def swap(array, axis, *others):
        other = lax.dynamic_index_in_dim(array, 1 - h, axis, keepdims=False)
        mine = lax.dynamic_index_in_dim(array, h, axis, keepdims=False)
        other = order.ran(order.after(other.astype(SENT), *others))
        return wide(mine) + wide(order.send(other, "y"))

    def ring_first(term, axis):
        up = order.ran(order.after(stack(low(term(2)), high(term(1)))))
        down = order.ran(order.after(stack(low(term(-1)), high(term(2)))))
        return order.send(up, axis + "+"), order.send(down, axis + "-")

    def ring_second(term, axis, first, *others):
        up, down = first
        value = (wide(low(term(1))) + wide(tie(low(up), *others))).astype(SENT)
        last_up = order.send(value, axis + "+")
        value = (wide(high(term(-1))) + wide(high(down))).astype(SENT)
        last_down = order.send(value, axis + "-")
        near, last = stack(low(down), high(up)), stack(last_up, last_down)
        return wide(term(0)) + wide(near) + wide(last)

    def direct_sum(term, axis, *others):
        up = order.send(term(1), axis + "+")
        far = order.send(tie(term(2), *others), axis + "2")
        down = order.send(tie(term(-1), *others), axis + "-")
        return (wide(term(0)) + wide(far)) + (wide(up) + wide(down))

    def total(part, halves):
        axis, sums = axes[part][1], []
        for half, way in zip(halves, "+-"):
            value = order.after(half) + wide(second[axis + way])
            sums.append(order.ran(value.astype(SENT)))
        return stack(*sums)

    sum_a = total(0, nears[0]).reshape(RING, BLOCK, WIDE)
    term_a = lambda k, s=sum_a: at(s, x + k)
    first_a = ring_first(term_a, "x")
    nears.append(near(1))
    drift = drift + order.send(tie(drift, got_c), "l", "rep")
    sum_c = (wide(got_c) + order.after(mine_c)).astype(SENT)
    sum_c = order.ran(sum_c).reshape(RING, 1024, NARROW)
    term_c = lambda k, s=sum_c: at(s, z + k)
    first_c = ring_first(term_c, "z")
    sum_b = total(1, nears[1]).reshape(RING, 2, 256, WIDE)
    sum_b = swap(sum_b, 1, drift).astype(SENT)
    sum_c = ring_second(term_c, "z", first_c).astype(SENT).reshape(RING, 256, NARROW)
    sum_a = ring_second(term_a, "x", first_a).reshape(2, 256, WIDE)
    drift = tie(drift, sum_b) / groups
    new_anchor, new_momentum, mix = outer_step(fragment, anchor, momentum, drift)

    grad_a = swap(sum_a, 0)
    grad_b = direct_sum(lambda k: at(sum_b, z + k), "z")
    grad_c = direct_sum(lambda k, s=sum_c: at(s, x + k), "x", grad_a)
    new_w, new_first, new_second = inner_step(
        fragment, grad_a, grad_b, grad_c,
        weights, first_moment[0], second_moment[0], mix,
    )
    return (new_w[None], new_first[None], new_second[None], new_anchor, new_momentum)


def solution(mesh):
    placed = (
        P(("rep", "fsdp"), None),
        P(("rep", "fsdp"), None),
        P("rep", "fsdp", None),
        P("rep", "fsdp", None),
        P("rep", "fsdp", None),
        P("fsdp", None),
        P("fsdp", None),
        P(),
    )
    return jax.shard_map(
        per_device,
        mesh=mesh,
        in_specs=placed,
        out_specs=(
            P("rep", "fsdp", None),
            P("rep", "fsdp", None),
            P("rep", "fsdp", None),
            P("fsdp", None),
            P("fsdp", None),
        ),
        check_vma=False,
    )
```

```python
import functools

import jax
import jax.numpy as jnp
from jax import lax
from jax.experimental import pallas as pl
from jax.experimental.pallas import tpu as pltpu
from jax.sharding import PartitionSpec as P

HEAD_DIM = 128
INNER_STEP = 100

beta_first = 0.9
beta_second = 0.95
epsilon = 1e-08
inner_rate = 0.00015
decay_rate = 0.1
outer_rate = 0.7
outer_factor = 0.9
mixing_share = 0.5

SENT = jnp.float16
WIDE, NARROW = 384, 256
RING = 4
TOK, ROWS = 768, 8192
BLOCK = 512
VMEM = 16 << 20


SHORT = pl.CostEstimate(flops=1, bytes_accessed=1, transcendentals=0)


def wide(value):
    return value.astype(jnp.float32)


def tie(value, *others):
    return lax.optimization_barrier((value, *others))[0]


def in_hbm(value):
    return pltpu.with_memory_space_constraint(value, pltpu.HBM)


SMEM_SPEC = pl.BlockSpec(memory_space=pltpu.SMEM)
VMEM_SPEC = pl.BlockSpec(memory_space=pltpu.VMEM)
ANY_SPEC = pl.BlockSpec(memory_space=pl.ANY)


def turned(left, right):
    return lax.dot_general(
        left, right, (((0,), (0,)), ((), ())), preferred_element_type=jnp.float32
    )


SLOTS = 3
PAIR = 2 * BLOCK


def streamed(acts, ids, held, sems, count):
    def copies(i):
        made = []
        for k in range(2):
            start = ids[2 * i + k] * BLOCK
            start = start if isinstance(start, int) else pl.multiple_of(start, BLOCK)
            source = acts.at[:, pl.ds(start, BLOCK)]
            target = held.at[i % SLOTS, :, k * BLOCK : (k + 1) * BLOCK]
            made.append(pltpu.make_async_copy(source, target, sems.at[i % SLOTS, k]))
        return made

    for i in range(min(SLOTS, count)):
        for copy in copies(i):
            copy.start()
    for i in range(count):
        for copy in copies(i):
            copy.wait()
        yield i, held.at[i % SLOTS]
        if i + SLOTS < count:
            for copy in copies(i + SLOTS):
                copy.start()


def rest_kernel(ids, acts, cots, *refs):
    relays, owns = refs[:4], refs[4:6]
    held, cots_here, own_here, sems, cots_sems, back_sems = refs[6:]
    copies = []
    for part in range(2):
        cut = slice(part * WIDE, (part + 1) * WIDE)
        copies.append(
            pltpu.make_async_copy(cots.at[:, cut], cots_here.at[:, cut], cots_sems.at[part])
        )
        copies[-1].start()
    back = []
    for i, left in streamed(acts, ids, held, sems, 8):
        part, k = i // 4, i % 4
        if k == 0:
            copies[part].wait()
        value = turned(left[...], cots_here[:, part * WIDE : (part + 1) * WIDE])
        if k < 2:
            relays[2 * part + k][...] = value
        else:
            slot, rows = 2 * part + k - 2, slice((k - 2) * PAIR, (k - 1) * PAIR)
            own_here[slot] = value
            copy = pltpu.make_async_copy(
                own_here.at[slot], owns[part].at[rows], back_sems.at[slot]
            )
            copy.start()
            back.append(copy)
    for copy in back:
        copy.wait()


def dot_rest(ids, acts, cots):
    return pl.pallas_call(
        rest_kernel,
        in_specs=[SMEM_SPEC, ANY_SPEC, ANY_SPEC],
        out_specs=[VMEM_SPEC] * 4 + [ANY_SPEC] * 2,
        out_shape=[pltpu.VMEM((PAIR, WIDE), jnp.float32)] * 4
        + [pltpu.HBM((2 * PAIR, WIDE), jnp.float32)] * 2,
        scratch_shapes=[
            pltpu.VMEM((SLOTS, TOK, PAIR), acts.dtype),
            pltpu.VMEM((TOK, 2 * WIDE), cots.dtype),
            pltpu.VMEM((4, PAIR, WIDE), jnp.float32),
            pltpu.SemaphoreType.DMA((SLOTS, 2)),
            pltpu.SemaphoreType.DMA((2,)),
            pltpu.SemaphoreType.DMA((4,)),
        ],
        compiler_params=pltpu.CompilerParams(vmem_limit_bytes=13 << 20),
        cost_estimate=SHORT,
        name="dot_rest",
    )(ids, in_hbm(acts), in_hbm(cots))


def first_kernel(ids, acts, cots, *refs):
    firsts, (held, cots_here, sems, cots_sems) = refs[:4], refs[4:]
    copies = []
    for part in range(2):
        cut = slice(part * WIDE, (part + 1) * WIDE)
        copies.append(
            pltpu.make_async_copy(cots.at[:, cut], cots_here.at[:, cut], cots_sems.at[part])
        )
        copies[-1].start()
    for i, left in streamed(acts, ids, held, sems, 8):
        part, row = i // 4, i % 2 * PAIR
        if i % 4 == 0:
            copies[part].wait()
        right = cots_here[:, part * WIDE : (part + 1) * WIDE]
        firsts[i // 2][row : row + PAIR] = turned(left[...], right)


def dot_first(ids, acts, cots):
    return pl.pallas_call(
        first_kernel,
        in_specs=[SMEM_SPEC, ANY_SPEC, ANY_SPEC],
        out_specs=[VMEM_SPEC] * 4,
        out_shape=[pltpu.VMEM((2 * PAIR, WIDE), jnp.float32)] * 4,
        scratch_shapes=[
            pltpu.VMEM((SLOTS, TOK, PAIR), acts.dtype),
            pltpu.VMEM((TOK, 2 * WIDE), cots.dtype),
            pltpu.SemaphoreType.DMA((SLOTS, 2)),
            pltpu.SemaphoreType.DMA((2,)),
        ],
        compiler_params=pltpu.CompilerParams(vmem_limit_bytes=10 << 20),
        cost_estimate=SHORT,
        name="dot_first",
    )(ids, in_hbm(acts), in_hbm(cots))


def pair_kernel(ids, acts, cots, mine, other, held, cots_here, mine_here, sems, own_sems):
    count, own = ROWS // PAIR, ids[0]
    copy = pltpu.make_async_copy(cots.at[:, 2 * WIDE :], cots_here, own_sems.at[count])
    copy.start()
    back = []
    for i, left in streamed(acts, range(2 * count), held, sems, count):
        if i == 0:
            copy.wait()
        for k in range(2):
            for to, side in ((mine_here, own), (other, 1 - own)):
                half = left[:, pl.ds(pl.multiple_of(k * BLOCK + side * 256, 256), 256)]
                to[i * 512 + k * 256 : i * 512 + (k + 1) * 256] = turned(half, cots_here[...])
        cut = pl.ds(i * 512, 512)
        back.append(pltpu.make_async_copy(mine_here.at[cut], mine.at[cut], own_sems.at[i]))
        back[-1].start()
    for copy in back:
        copy.wait()


def dot_pairs(ids, acts, cots):
    count = ROWS // PAIR
    return pl.pallas_call(
        pair_kernel,
        in_specs=[SMEM_SPEC, ANY_SPEC, ANY_SPEC],
        out_specs=[ANY_SPEC, VMEM_SPEC],
        out_shape=[
            pltpu.HBM((ROWS // 2, NARROW), jnp.float32),
            pltpu.VMEM((ROWS // 2, NARROW), jnp.float32),
        ],
        scratch_shapes=[
            pltpu.VMEM((SLOTS, TOK, PAIR), acts.dtype),
            pltpu.VMEM((TOK, NARROW), cots.dtype),
            pltpu.VMEM((ROWS // 2, NARROW), jnp.float32),
            pltpu.SemaphoreType.DMA((SLOTS, 2)),
            pltpu.SemaphoreType.DMA((1 + count,)),
        ],
        compiler_params=pltpu.CompilerParams(vmem_limit_bytes=10 << 20),
        cost_estimate=SHORT,
        name="dot_pairs",
    )(ids, in_hbm(acts), in_hbm(cots))


AXES = ("rep", "fsdp")


def pairs_of(dz=0, dx=0, dh=0, dl=0, dc=0):
    place = lambda z, x, h, l, c: ((l * 2 + c) * RING + z) * RING * 2 + x * 2 + h
    return [
        (
            place(z, x, h, l, c),
            place((z + dz) % RING, (x + dx) % RING, (h + dh) % 2, (l + dl) % 2, (c + dc) % 2),
        )
        for z in range(RING)
        for x in range(RING)
        for h in range(2)
        for l in range(2)
        for c in range(2)
    ]


CHANNELS = {
    "z+": dict(dz=1),
    "z-": dict(dz=-1),
    "x+": dict(dx=1),
    "x-": dict(dx=-1),
    "z2": dict(dz=2),
    "x2": dict(dx=2),
    "y": dict(dh=1),
    "l": dict(dl=1),
    "c": dict(dc=1),
}


class Order:
    def __init__(self):
        self.arrived = {}
        self.last = None

    def after(self, value, *others):
        return value if self.last is None else tie(value, self.last, *others)

    def ran(self, value):
        self.last = value
        return value

    def send(self, value, step, channel=None):
        channel = channel or step
        if channel in self.arrived:
            value = tie(value, self.arrived[channel])
        got = lax.ppermute(value, AXES, pairs_of(**CHANNELS[step]))
        self.arrived[channel] = got
        return got


def outer_kernel(fragment, anchor, momentum, drift, new_anchor, new_momentum, mix):
    outer = drift[...]
    for k in range(anchor.shape[1] // HEAD_DIM):
        cut = slice(k * HEAD_DIM, (k + 1) * HEAD_DIM)
        chosen = fragment[0] == k
        momentum_part = outer_factor * momentum[:, cut] + outer
        anchor_next = anchor[:, cut] - outer_rate * (outer + outer_factor * momentum_part)
        new_momentum[:, cut] = jnp.where(chosen, momentum_part, momentum[:, cut])
        new_anchor[:, cut] = jnp.where(chosen, anchor_next, anchor[:, cut])

        @pl.when(chosen)
        def _():
            mix[...] = (1.0 - mixing_share) * anchor_next


def outer_step(fragment, anchor, momentum, drift):
    rows, cols = anchor.shape
    step = 64
    full = pl.BlockSpec((step, cols), lambda i, fragment: (i, 0))
    head = pl.BlockSpec((step, HEAD_DIM), lambda i, fragment: (i, 0))
    return pl.pallas_call(
        outer_kernel,
        grid_spec=pltpu.PrefetchScalarGridSpec(
            num_scalar_prefetch=1,
            grid=(rows // step,),
            in_specs=[full, full, head],
            out_specs=[full, full, head],
        ),
        out_shape=[
            jax.ShapeDtypeStruct(anchor.shape, jnp.float32),
            jax.ShapeDtypeStruct(anchor.shape, jnp.float32),
            jax.ShapeDtypeStruct((rows, HEAD_DIM), jnp.float32),
        ],
        compiler_params=pltpu.CompilerParams(vmem_limit_bytes=VMEM),
        cost_estimate=SHORT,
        name="outer_step",
    )(fragment, anchor, momentum, drift)


def inner_kernel(fragment, grad_a, grad_b, grad_c, weights, first, second, mix, *outs):
    new_w, new_first, new_second = outs
    for k in range(weights.shape[1] // HEAD_DIM):
        cut = slice(k * HEAD_DIM, (k + 1) * HEAD_DIM)
        part = (grad_a, grad_b, grad_c)[k // 3]
        grad = part[:, k % 3 * HEAD_DIM : (k % 3 + 1) * HEAD_DIM]
        moment = beta_first * first[:, cut] + (1.0 - beta_first) * grad
        square = beta_second * second[:, cut] + (1.0 - beta_second) * grad * grad
        new_first[:, cut] = moment
        new_second[:, cut] = square
        update = (
            moment
            / (1.0 - beta_first**INNER_STEP)
            / (jnp.sqrt(square / (1.0 - beta_second**INNER_STEP)) + epsilon)
        )
        stepped = weights[:, cut] - inner_rate * (update + decay_rate * weights[:, cut])
        mixed = mixing_share * stepped + mix[...]
        new_w[:, cut] = jnp.where(fragment[0] == k, mixed, stepped)


def inner_step(fragment, grad_a, grad_b, grad_c, weights, first, second, mix):
    rows, cols = weights.shape
    step = 64
    block = lambda width: pl.BlockSpec((step, width), lambda i, fragment: (i, 0))
    full, head = block(cols), block(HEAD_DIM)
    return pl.pallas_call(
        inner_kernel,
        grid_spec=pltpu.PrefetchScalarGridSpec(
            num_scalar_prefetch=1,
            grid=(rows // step,),
            in_specs=[block(WIDE), block(WIDE), block(NARROW), full, full, full, head],
            out_specs=[full] * 3,
        ),
        out_shape=[jax.ShapeDtypeStruct(weights.shape, jnp.float32)] * 3,
        compiler_params=pltpu.CompilerParams(vmem_limit_bytes=VMEM),
        cost_estimate=SHORT,
        name="inner_step",
    )(fragment, grad_a, grad_b, grad_c, weights, first, second, mix)


def low(value):
    return value[: value.shape[0] // 2]


def high(value):
    return value[value.shape[0] // 2 :]


def stack(upper, lower):
    return jnp.concatenate([upper, lower], 0)


def per_device(acts, cots, inner_w, first_moment, second_moment, anchor, momentum, fragment):
    span = HEAD_DIM
    me = lax.axis_index("fsdp").astype(jnp.int32)
    z, x, h = me >> 3, (me >> 1) & 3, me & 1
    order = Order()

    def blocks(part, quarters):
        ids = []
        for offset, half in quarters:
            for k in (2 * half, 2 * half + 1):
                if part == 0:
                    ids.append((((z + offset) & 3) << 2) + k)
                else:
                    ids.append((k << 2) + ((x + offset) & 3))
        return ids

    axes = ((0, "z"), (1, "x"))
    first, second, relayed = {}, {}, {}
    ids = blocks(0, [(2, 0), (1, 1), (-1, 0), (2, 1)])
    ids += blocks(1, [(2, 0), (1, 1), (-1, 0), (2, 1)])
    terms = dot_first(jnp.stack(ids), acts, cots)
    for term, channel in zip(terms, ("z+", "z-", "x+", "x-")):
        term = order.ran(order.after(term).astype(SENT))
        first[channel] = order.send(term, channel)

    weights = inner_w[0]
    column = fragment[0] * span
    groups = lax.axis_size("rep")
    cut = lambda v: lax.dynamic_slice_in_dim(v, column, span, 1)
    drift = order.after(cut(anchor) - cut(weights))
    drift = drift + order.send(drift, "c", "rep")

    mine_c, other_c = dot_pairs(order.after(h.reshape(1)), acts, cots)
    other_c = order.ran(tie(other_c, order.last, drift).astype(SENT))
    got_c = order.send(other_c, "y")

    ids = []
    for part, axis in axes:
        ids += blocks(part, [(1, 0), (-1, 1), (0, 0), (0, 1)])
    *terms, own_a, own_b = dot_rest(order.after(jnp.stack(ids)), acts, cots)
    order.ran(terms[0])
    relayed.update(zip(("z+", "z-", "x+", "x-"), terms))
    own = own_a, own_b

    def near(part, *others):
        axis = axes[part][1]
        halves = []
        for half, way in ((low, "-"), (high, "+")):
            value = order.after(half(own[part]), *others) + wide(half(first[axis + way]))
            halves.append(order.ran(value))
        return halves

    nears = []
    for part, axis in axes:
        term = order.after(relayed[axis + "+"]) + wide(low(first[axis + "+"]))
        second[axis + "+"] = order.send(order.ran(term.astype(SENT)), axis + "+")
        term = order.after(relayed[axis + "-"]) + wide(high(first[axis + "-"]))
        second[axis + "-"] = order.send(order.ran(term.astype(SENT)), axis + "-")

    def at(array, position, axis=0):
        return lax.dynamic_index_in_dim(array, position & 3, axis, keepdims=False)

    def swap(array, axis, *others):
        other = lax.dynamic_index_in_dim(array, 1 - h, axis, keepdims=False)
        mine = lax.dynamic_index_in_dim(array, h, axis, keepdims=False)
        other = order.ran(order.after(other.astype(SENT), *others))
        return wide(mine) + wide(order.send(other, "y"))

    def ring_first(term, axis):
        up = order.ran(order.after(stack(low(term(2)), high(term(1)))))
        down = order.ran(order.after(stack(low(term(-1)), high(term(2)))))
        return order.send(up, axis + "+"), order.send(down, axis + "-")

    def ring_second(term, axis, first, *others):
        up, down = first
        value = (wide(low(term(1))) + wide(tie(low(up), *others))).astype(SENT)
        last_up = order.send(value, axis + "+")
        value = (wide(high(term(-1))) + wide(high(down))).astype(SENT)
        last_down = order.send(value, axis + "-")
        near, last = stack(low(down), high(up)), stack(last_up, last_down)
        return wide(term(0)) + wide(near) + wide(last)

    def direct_sum(term, axis, *others):
        up = order.send(term(1), axis + "+")
        far = order.send(tie(term(2), *others), axis + "2")
        down = order.send(tie(term(-1), *others), axis + "-")
        return (wide(term(0)) + wide(far)) + (wide(up) + wide(down))

    def total(part, halves):
        axis, sums = axes[part][1], []
        for half, way in zip(halves, "+-"):
            value = order.after(half) + wide(second[axis + way])
            sums.append(order.ran(value.astype(SENT)))
        return stack(*sums)

    nears.append(near(0, second["z+"]))
    sum_a = total(0, nears[0]).reshape(RING, BLOCK, WIDE)
    term_a = lambda k, s=sum_a: at(s, x + k)
    first_a = ring_first(term_a, "x")
    nears.append(near(1))
    sum_b = total(1, nears[1]).reshape(RING, 2, 256, WIDE)
    sum_b = swap(sum_b, 1).astype(SENT)
    sum_c = (wide(got_c) + order.after(mine_c)).astype(SENT)
    sum_c = order.ran(sum_c).reshape(RING, 1024, NARROW)
    term_c = lambda k, s=sum_c: at(s, z + k)
    first_c = ring_first(term_c, "z")
    sum_c = ring_second(term_c, "z", first_c).astype(SENT).reshape(RING, 256, NARROW)
    sum_a = ring_second(term_a, "x", first_a).reshape(2, 256, WIDE)
    drift = drift + order.send(tie(drift, sum_b), "l", "rep")
    new_anchor, new_momentum, mix = outer_step(fragment, anchor, momentum, drift / groups)

    grad_a = swap(sum_a, 0)
    grad_b = direct_sum(lambda k: at(sum_b, z + k), "z")
    grad_c = direct_sum(lambda k, s=tie(sum_c, grad_a): at(s, x + k), "x")
    new_w, new_first, new_second = inner_step(
        fragment, grad_a, grad_b, grad_c,
        weights, first_moment[0], second_moment[0], mix,
    )
    return (new_w[None], new_first[None], new_second[None], new_anchor, new_momentum)


def solution(mesh):
    placed = (
        P(("rep", "fsdp"), None),
        P(("rep", "fsdp"), None),
        P("rep", "fsdp", None),
        P("rep", "fsdp", None),
        P("rep", "fsdp", None),
        P("fsdp", None),
        P("fsdp", None),
        P(),
    )
    return jax.shard_map(
        per_device,
        mesh=mesh,
        in_specs=placed,
        out_specs=(
            P("rep", "fsdp", None),
            P("rep", "fsdp", None),
            P("rep", "fsdp", None),
            P("fsdp", None),
            P("fsdp", None),
        ),
        check_vma=False,
    )
```

```python
import functools

import jax
import jax.numpy as jnp
from jax import lax
from jax.experimental import pallas as pl
from jax.experimental.pallas import tpu as pltpu
from jax.sharding import PartitionSpec as P

HEAD_DIM = 128
INNER_STEP = 100

beta_first = 0.9
beta_second = 0.95
epsilon = 1e-08
inner_rate = 0.00015
decay_rate = 0.1
outer_rate = 0.7
outer_factor = 0.9
mixing_share = 0.5

SENT = jnp.float16
WIDE, NARROW = 384, 256
RING = 4
TOK, ROWS = 768, 8192
BLOCK = 512
VMEM = 16 << 20


SHORT = pl.CostEstimate(flops=1, bytes_accessed=1, transcendentals=0)


def wide(value):
    return value.astype(jnp.float32)


def tie(value, *others):
    return lax.optimization_barrier((value, *others))[0]


def in_hbm(value):
    return pltpu.with_memory_space_constraint(value, pltpu.HBM)


SMEM_SPEC = pl.BlockSpec(memory_space=pltpu.SMEM)
VMEM_SPEC = pl.BlockSpec(memory_space=pltpu.VMEM)
ANY_SPEC = pl.BlockSpec(memory_space=pl.ANY)


def turned(left, right):
    return lax.dot_general(
        left, right, (((0,), (0,)), ((), ())), preferred_element_type=jnp.float32
    )


SLOTS = 3
PAIR = 2 * BLOCK


def streamed(acts, ids, held, sems, count):
    def copies(i):
        made = []
        for k in range(2):
            start = ids[2 * i + k] * BLOCK
            start = start if isinstance(start, int) else pl.multiple_of(start, BLOCK)
            source = acts.at[:, pl.ds(start, BLOCK)]
            target = held.at[i % SLOTS, :, k * BLOCK : (k + 1) * BLOCK]
            made.append(pltpu.make_async_copy(source, target, sems.at[i % SLOTS, k]))
        return made

    for i in range(min(SLOTS, count)):
        for copy in copies(i):
            copy.start()
    for i in range(count):
        for copy in copies(i):
            copy.wait()
        yield i, held.at[i % SLOTS]
        if i + SLOTS < count:
            for copy in copies(i + SLOTS):
                copy.start()


def rest_kernel(ids, acts, cots, *refs):
    relays, owns = refs[:4], refs[4:6]
    held, cots_here, own_here, sems, cots_sems, back_sems = refs[6:]
    copies = []
    for part in range(2):
        cut = slice(part * WIDE, (part + 1) * WIDE)
        copies.append(
            pltpu.make_async_copy(cots.at[:, cut], cots_here.at[:, cut], cots_sems.at[part])
        )
        copies[-1].start()
    back = []
    for i, left in streamed(acts, ids, held, sems, 8):
        part, k = i // 4, i % 4
        if k == 0:
            copies[part].wait()
        value = turned(left[...], cots_here[:, part * WIDE : (part + 1) * WIDE])
        if k < 2:
            relays[2 * part + k][...] = value
        else:
            slot, rows = 2 * part + k - 2, slice((k - 2) * PAIR, (k - 1) * PAIR)
            own_here[slot] = value
            copy = pltpu.make_async_copy(
                own_here.at[slot], owns[part].at[rows], back_sems.at[slot]
            )
            copy.start()
            back.append(copy)
    for copy in back:
        copy.wait()


def dot_rest(ids, acts, cots):
    return pl.pallas_call(
        rest_kernel,
        in_specs=[SMEM_SPEC, ANY_SPEC, ANY_SPEC],
        out_specs=[VMEM_SPEC] * 4 + [ANY_SPEC] * 2,
        out_shape=[pltpu.VMEM((PAIR, WIDE), jnp.float32)] * 4
        + [pltpu.HBM((2 * PAIR, WIDE), jnp.float32)] * 2,
        scratch_shapes=[
            pltpu.VMEM((SLOTS, TOK, PAIR), acts.dtype),
            pltpu.VMEM((TOK, 2 * WIDE), cots.dtype),
            pltpu.VMEM((4, PAIR, WIDE), jnp.float32),
            pltpu.SemaphoreType.DMA((SLOTS, 2)),
            pltpu.SemaphoreType.DMA((2,)),
            pltpu.SemaphoreType.DMA((4,)),
        ],
        compiler_params=pltpu.CompilerParams(vmem_limit_bytes=13 << 20),
        cost_estimate=SHORT,
        name="dot_rest",
    )(ids, in_hbm(acts), in_hbm(cots))


def first_kernel(ids, acts, cots, *refs):
    firsts, (held, cots_here, sems, cots_sems) = refs[:4], refs[4:]
    copies = []
    for part in range(2):
        cut = slice(part * WIDE, (part + 1) * WIDE)
        copies.append(
            pltpu.make_async_copy(cots.at[:, cut], cots_here.at[:, cut], cots_sems.at[part])
        )
        copies[-1].start()
    for i, left in streamed(acts, ids, held, sems, 8):
        part, row = i // 4, i % 2 * PAIR
        if i % 4 == 0:
            copies[part].wait()
        right = cots_here[:, part * WIDE : (part + 1) * WIDE]
        firsts[i // 2][row : row + PAIR] = turned(left[...], right)


def dot_first(ids, acts, cots):
    return pl.pallas_call(
        first_kernel,
        in_specs=[SMEM_SPEC, ANY_SPEC, ANY_SPEC],
        out_specs=[VMEM_SPEC] * 4,
        out_shape=[pltpu.VMEM((2 * PAIR, WIDE), jnp.float32)] * 4,
        scratch_shapes=[
            pltpu.VMEM((SLOTS, TOK, PAIR), acts.dtype),
            pltpu.VMEM((TOK, 2 * WIDE), cots.dtype),
            pltpu.SemaphoreType.DMA((SLOTS, 2)),
            pltpu.SemaphoreType.DMA((2,)),
        ],
        compiler_params=pltpu.CompilerParams(vmem_limit_bytes=10 << 20),
        cost_estimate=SHORT,
        name="dot_first",
    )(ids, in_hbm(acts), in_hbm(cots))


def pair_kernel(ids, acts, cots, mine, other, held, cots_here, here, sems, own_sems):
    count, own = ROWS // PAIR, ids[0]
    copy = pltpu.make_async_copy(cots.at[:, 2 * WIDE :], cots_here, own_sems.at[2 * count])
    copy.start()
    back = []
    for i, left in streamed(acts, range(2 * count), held, sems, count):
        if i == 0:
            copy.wait()
        for k in range(2):
            for to, side in ((0, own), (1, 1 - own)):
                half = left[:, pl.ds(pl.multiple_of(k * BLOCK + side * 256, 256), 256)]
                here[to, i * 512 + k * 256 : i * 512 + (k + 1) * 256] = turned(half, cots_here[...])
        cut = pl.ds(i * 512, 512)
        for to, whole in ((1, other), (0, mine)):
            sem = own_sems.at[to * count + i]
            back.append(pltpu.make_async_copy(here.at[to, cut], whole.at[cut], sem))
            back[-1].start()
    for copy in back:
        copy.wait()


def dot_pairs(ids, acts, cots):
    count = ROWS // PAIR
    return pl.pallas_call(
        pair_kernel,
        in_specs=[SMEM_SPEC, ANY_SPEC, ANY_SPEC],
        out_specs=[ANY_SPEC, ANY_SPEC],
        out_shape=[
            pltpu.HBM((ROWS // 2, NARROW), jnp.float32),
            pltpu.HBM((ROWS // 2, NARROW), jnp.float32),
        ],
        scratch_shapes=[
            pltpu.VMEM((SLOTS, TOK, PAIR), acts.dtype),
            pltpu.VMEM((TOK, NARROW), cots.dtype),
            pltpu.VMEM((2, ROWS // 2, NARROW), jnp.float32),
            pltpu.SemaphoreType.DMA((SLOTS, 2)),
            pltpu.SemaphoreType.DMA((1 + 2 * count,)),
        ],
        compiler_params=pltpu.CompilerParams(vmem_limit_bytes=15 << 20),
        cost_estimate=SHORT,
        name="dot_pairs",
    )(ids, in_hbm(acts), in_hbm(cots))


AXES = ("rep", "fsdp")


def pairs_of(dz=0, dx=0, dh=0, dl=0, dc=0):
    place = lambda z, x, h, l, c: ((l * 2 + c) * RING + z) * RING * 2 + x * 2 + h
    return [
        (
            place(z, x, h, l, c),
            place((z + dz) % RING, (x + dx) % RING, (h + dh) % 2, (l + dl) % 2, (c + dc) % 2),
        )
        for z in range(RING)
        for x in range(RING)
        for h in range(2)
        for l in range(2)
        for c in range(2)
    ]


CHANNELS = {
    "z+": dict(dz=1),
    "z-": dict(dz=-1),
    "x+": dict(dx=1),
    "x-": dict(dx=-1),
    "z2": dict(dz=2),
    "x2": dict(dx=2),
    "y": dict(dh=1),
    "l": dict(dl=1),
    "c": dict(dc=1),
}


class Order:
    def __init__(self):
        self.arrived = {}
        self.last = None

    def after(self, value, *others):
        return value if self.last is None else tie(value, self.last, *others)

    def ran(self, value):
        self.last = value
        return value

    def send(self, value, step, channel=None):
        channel = channel or step
        if channel in self.arrived:
            value = tie(value, self.arrived[channel])
        got = lax.ppermute(value, AXES, pairs_of(**CHANNELS[step]))
        self.arrived[channel] = got
        return got


def outer_kernel(fragment, anchor, momentum, drift, new_anchor, new_momentum, mix):
    outer = drift[...]
    for k in range(anchor.shape[1] // HEAD_DIM):
        cut = slice(k * HEAD_DIM, (k + 1) * HEAD_DIM)
        chosen = fragment[0] == k
        momentum_part = outer_factor * momentum[:, cut] + outer
        anchor_next = anchor[:, cut] - outer_rate * (outer + outer_factor * momentum_part)
        new_momentum[:, cut] = jnp.where(chosen, momentum_part, momentum[:, cut])
        new_anchor[:, cut] = jnp.where(chosen, anchor_next, anchor[:, cut])

        @pl.when(chosen)
        def _():
            mix[...] = (1.0 - mixing_share) * anchor_next


def outer_step(fragment, anchor, momentum, drift):
    rows, cols = anchor.shape
    step = 64
    full = pl.BlockSpec((step, cols), lambda i, fragment: (i, 0))
    head = pl.BlockSpec((step, HEAD_DIM), lambda i, fragment: (i, 0))
    return pl.pallas_call(
        outer_kernel,
        grid_spec=pltpu.PrefetchScalarGridSpec(
            num_scalar_prefetch=1,
            grid=(rows // step,),
            in_specs=[full, full, head],
            out_specs=[full, full, head],
        ),
        out_shape=[
            jax.ShapeDtypeStruct(anchor.shape, jnp.float32),
            jax.ShapeDtypeStruct(anchor.shape, jnp.float32),
            jax.ShapeDtypeStruct((rows, HEAD_DIM), jnp.float32),
        ],
        compiler_params=pltpu.CompilerParams(vmem_limit_bytes=VMEM),
        cost_estimate=SHORT,
        name="outer_step",
    )(fragment, anchor, momentum, drift)


def inner_kernel(fragment, grad_a, grad_b, grad_c, weights, first, second, mix, *outs):
    new_w, new_first, new_second = outs
    for k in range(weights.shape[1] // HEAD_DIM):
        cut = slice(k * HEAD_DIM, (k + 1) * HEAD_DIM)
        part = (grad_a, grad_b, grad_c)[k // 3]
        grad = part[:, k % 3 * HEAD_DIM : (k % 3 + 1) * HEAD_DIM]
        moment = beta_first * first[:, cut] + (1.0 - beta_first) * grad
        square = beta_second * second[:, cut] + (1.0 - beta_second) * grad * grad
        new_first[:, cut] = moment
        new_second[:, cut] = square
        update = (
            moment
            / (1.0 - beta_first**INNER_STEP)
            / (jnp.sqrt(square / (1.0 - beta_second**INNER_STEP)) + epsilon)
        )
        stepped = weights[:, cut] - inner_rate * (update + decay_rate * weights[:, cut])
        mixed = mixing_share * stepped + mix[...]
        new_w[:, cut] = jnp.where(fragment[0] == k, mixed, stepped)


def inner_step(fragment, grad_a, grad_b, grad_c, weights, first, second, mix):
    rows, cols = weights.shape
    step = 128
    block = lambda width: pl.BlockSpec((step, width), lambda i, fragment: (i, 0))
    full, head = block(cols), block(HEAD_DIM)
    return pl.pallas_call(
        inner_kernel,
        grid_spec=pltpu.PrefetchScalarGridSpec(
            num_scalar_prefetch=1,
            grid=(rows // step,),
            in_specs=[block(WIDE), block(WIDE), block(NARROW), full, full, full, head],
            out_specs=[full] * 3,
        ),
        out_shape=[jax.ShapeDtypeStruct(weights.shape, jnp.float32)] * 3,
        compiler_params=pltpu.CompilerParams(vmem_limit_bytes=VMEM),
        cost_estimate=SHORT,
        name="inner_step",
    )(fragment, grad_a, grad_b, grad_c, weights, first, second, mix)


def low(value):
    return value[: value.shape[0] // 2]


def high(value):
    return value[value.shape[0] // 2 :]


def stack(upper, lower):
    return jnp.concatenate([upper, lower], 0)


def per_device(acts, cots, inner_w, first_moment, second_moment, anchor, momentum, fragment):
    span = HEAD_DIM
    me = lax.axis_index("fsdp").astype(jnp.int32)
    z, x, h = me >> 3, (me >> 1) & 3, me & 1
    order = Order()

    def blocks(part, quarters):
        ids = []
        for offset, half in quarters:
            for k in (2 * half, 2 * half + 1):
                if part == 0:
                    ids.append((((z + offset) & 3) << 2) + k)
                else:
                    ids.append((k << 2) + ((x + offset) & 3))
        return ids

    axes = ((0, "z"), (1, "x"))
    first, second, relayed = {}, {}, {}
    ids = blocks(0, [(2, 0), (1, 1), (-1, 0), (2, 1)])
    ids += blocks(1, [(2, 0), (1, 1), (-1, 0), (2, 1)])
    terms = dot_first(jnp.stack(ids), acts, cots)
    for term, channel in zip(terms, ("z+", "z-", "x+", "x-")):
        term = order.ran(order.after(term).astype(SENT))
        first[channel] = order.send(term, channel)

    weights = inner_w[0]
    column = fragment[0] * span
    groups = lax.axis_size("rep")
    cut = lambda v: lax.dynamic_slice_in_dim(v, column, span, 1)
    drift = order.after(cut(anchor) - cut(weights))
    drift = drift + order.send(drift, "c", "rep")

    mine_c, other_c = dot_pairs(order.after(h.reshape(1)), acts, cots)
    other_c = order.ran(tie(other_c, order.last, drift).astype(SENT))
    got_c = order.send(other_c, "y")

    ids = []
    for part, axis in axes:
        ids += blocks(part, [(1, 0), (-1, 1), (0, 0), (0, 1)])
    *terms, own_a, own_b = dot_rest(order.after(jnp.stack(ids)), acts, cots)
    order.ran(terms[0])
    relayed.update(zip(("z+", "z-", "x+", "x-"), terms))
    own = own_a, own_b

    def near(part, *others):
        axis = axes[part][1]
        halves = []
        for half, way in ((low, "-"), (high, "+")):
            value = order.after(half(own[part]), *others) + wide(half(first[axis + way]))
            halves.append(order.ran(value))
        return halves

    nears = []
    for part, axis in axes:
        term = order.after(relayed[axis + "+"]) + wide(low(first[axis + "+"]))
        second[axis + "+"] = order.send(order.ran(term.astype(SENT)), axis + "+")
        term = order.after(relayed[axis + "-"]) + wide(high(first[axis + "-"]))
        second[axis + "-"] = order.send(order.ran(term.astype(SENT)), axis + "-")

    def at(array, position, axis=0):
        return lax.dynamic_index_in_dim(array, position & 3, axis, keepdims=False)

    def swap(array, axis, *others):
        other = lax.dynamic_index_in_dim(array, 1 - h, axis, keepdims=False)
        mine = lax.dynamic_index_in_dim(array, h, axis, keepdims=False)
        other = order.ran(order.after(other.astype(SENT), *others))
        return wide(mine) + wide(order.send(other, "y"))

    def ring_first(term, axis):
        up = order.ran(order.after(stack(low(term(2)), high(term(1)))))
        down = order.ran(order.after(stack(low(term(-1)), high(term(2)))))
        return order.send(up, axis + "+"), order.send(down, axis + "-")

    def ring_second(term, axis, first, *others):
        up, down = first
        value = (wide(low(term(1))) + wide(tie(low(up), *others))).astype(SENT)
        last_up = order.send(value, axis + "+")
        value = (wide(high(term(-1))) + wide(high(down))).astype(SENT)
        last_down = order.send(value, axis + "-")
        near, last = stack(low(down), high(up)), stack(last_up, last_down)
        return wide(term(0)) + wide(near) + wide(last)

    def direct_sum(term, axis, *others):
        up = order.send(term(1), axis + "+")
        far = order.send(tie(term(2), *others), axis + "2")
        down = order.send(tie(term(-1), *others), axis + "-")
        return (wide(term(0)) + wide(far)) + (wide(up) + wide(down))

    def total(part, halves):
        axis, sums = axes[part][1], []
        for half, way in zip(halves, "+-"):
            value = order.after(half) + wide(second[axis + way])
            sums.append(order.ran(value.astype(SENT)))
        return stack(*sums)

    nears.append(near(0, second["z+"]))
    sum_a = total(0, nears[0]).reshape(RING, BLOCK, WIDE)
    term_a = lambda k, s=sum_a: at(s, x + k)
    first_a = ring_first(term_a, "x")
    nears.append(near(1))
    sum_b = total(1, nears[1]).reshape(RING, 2, 256, WIDE)
    sum_b = swap(sum_b, 1).astype(SENT)
    sum_c = (wide(got_c) + order.after(mine_c)).astype(SENT)
    sum_c = order.ran(sum_c).reshape(RING, 1024, NARROW)
    term_c = lambda k, s=sum_c: at(s, z + k)
    first_c = ring_first(term_c, "z")
    sum_c = ring_second(term_c, "z", first_c).astype(SENT).reshape(RING, 256, NARROW)
    sum_a = ring_second(term_a, "x", first_a).reshape(2, 256, WIDE)
    drift = drift + order.send(tie(drift, sum_b), "l", "rep")
    new_anchor, new_momentum, mix = outer_step(fragment, anchor, momentum, drift / groups)

    grad_a = swap(sum_a, 0)
    grad_b = direct_sum(lambda k: at(sum_b, z + k), "z")
    grad_c = direct_sum(lambda k, s=tie(sum_c, grad_a): at(s, x + k), "x")
    new_w, new_first, new_second = inner_step(
        fragment, grad_a, grad_b, grad_c,
        weights, first_moment[0], second_moment[0], mix,
    )
    return (new_w[None], new_first[None], new_second[None], new_anchor, new_momentum)


def solution(mesh):
    placed = (
        P(("rep", "fsdp"), None),
        P(("rep", "fsdp"), None),
        P("rep", "fsdp", None),
        P("rep", "fsdp", None),
        P("rep", "fsdp", None),
        P("fsdp", None),
        P("fsdp", None),
        P(),
    )
    return jax.shard_map(
        per_device,
        mesh=mesh,
        in_specs=placed,
        out_specs=(
            P("rep", "fsdp", None),
            P("rep", "fsdp", None),
            P("rep", "fsdp", None),
            P("fsdp", None),
            P("fsdp", None),
        ),
        check_vma=False,
    )
```
